512 devices in a mesh: group: 8 (over x, core), rank: 64 (over z, y).
Axes of the slice: x: 4, y: 4, z: 16, core: 2. Of those that a mesh axis runs over, the one named last changes fastest.
Arguments:
- degree: int32 [65536], P(('group', 'rank')), may hold values from 2 to 5
- curve_order: int32 [512, 128], P(('group', 'rank')), may hold values from 0 to 127, each once within a row
- neighbours: int32 [6, 65536], P(None, ('group', 'rank')), may hold values from 0 to 65535, as said below
- coupling: float32 [6, 65536], P(None, ('group', 'rank')), may hold values from 0.03 to 0.2
- stiffness: float32 [65536], P(('group', 'rank')), may hold values from 0.1 to 1
- lame: float32 [65536], P(('group', 'rank')), may hold values from 0.05 to 0.5
- load: float32 [3, 6, 6, 6, 65536], P(None, None, None, None, ('group', 'rank')), may hold values from -6 to 6
Outputs:
- owner: int32 [65536], P(('group', 'rank'))
- smoothed: float32 [3, 6, 6, 6, 65536], P(None, None, None, None, ('group', 'rank'))
The draws below stay inside these ranges and needn't reach their ends.
Inputs may be any that keep to these rules, and one draw needn't show every extreme that they name: `curve_order`: every row is a permutation of 0 to 127. `neighbours`: each listed neighbour lies 1 to 32 positions away along the curve from its cell; every cell's first listed neighbour lies exactly 32 positions away.
All inputs are finite; a program needn't handle non-finite values.
Results may differ from the reference program's by a relative error of at most 0.0003.
Values sent between devices are 32-bit elements; how exact they have to be, the bound alone decides.
No kernel may reach another device: no remote copies, remote signals or barrier semaphores. Data moves between devices by JAX's collectives and lax.ppermute only.
A program may use at most 128 MiB of HBM per device.

```python
import math
import jax
import jax.numpy as jnp
from jax import lax

CELLS_DEV = 128
NODES = 6
COMPONENTS = 3
NB = 6
REACH = 32
SWEEPS = 2
DEGREE = 3
NCELLS = 65536
N_GROUP = 8
N_RANK = 64


def draw_neighbours(key, part):
    key = jax.random.fold_in(key, 11)
    first_key, second_key = jax.random.split(key)
    sizes = jax.random.randint(first_key, (NB, NCELLS), 1, REACH + 1)
    rows = jnp.arange(NB, dtype=jnp.int32)[:, None]
    sizes = jnp.where(rows == 0, REACH, sizes).astype(jnp.int32)
    signs = (jax.random.randint(second_key, (NB, NCELLS), 0, 2) * 2 - 1).astype(jnp.int32)
    cells = jnp.arange(NCELLS, dtype=jnp.int32)[None, :]
    target = cells + signs * sizes
    outside = (target < 0) | (target >= NCELLS)
    return jnp.where(outside, cells - signs * sizes, target).astype(jnp.int32)


def with_ends(array, stream_key, smallest, top_value):
    dims = array.shape
    index_at = [jax.random.randint(jax.random.fold_in(stream_key, axis), (), 0, dims[axis]) for axis in range(len(dims))]
    array = array.at[tuple(index_at)].set(smallest)
    longest = dims.index(max(dims))
    index_at[longest] = (index_at[longest] + 1) % dims[longest]
    return array.at[tuple(index_at)].set(top_value)


def level_of(own_key, extent, pieces, least, top_value):
    gain = 1.0
    for axis_at, shards_of in pieces:
        draws = jax.random.uniform(jax.random.fold_in(jax.random.fold_in(own_key, 6), axis_at), (shards_of,), jnp.float32, least / len(pieces), top_value / len(pieces))
        gain = gain * jnp.repeat(jnp.exp(draws), extent[axis_at] // shards_of).reshape((-1,) + (1,) * (len(extent) - 1 - axis_at))
    return gain


def centred(key, extent, spread, most, shards=(), kind=jnp.bfloat16):
    loudness = level_of(key, extent, shards, -0.22, 0.18) if shards else 1.0
    result = jax.random.normal(key, extent, jnp.float32) * spread * loudness
    return jnp.minimum(jnp.maximum(result, -most), most).astype(kind)


def setup_inputs(seed: int = 0) -> dict:
    splits = jax.random.split(jax.random.key(seed), 8)
    degree = with_ends(jax.random.randint(splits[0], (NCELLS,), 2, 6), jax.random.fold_in(splits[0], 1), 2, 5).astype(jnp.int32)
    curve_order = jax.vmap(lambda own: jax.random.permutation(own, CELLS_DEV))(jax.random.split(splits[1], (N_GROUP * N_RANK))).reshape((N_GROUP * N_RANK, CELLS_DEV)).astype(jnp.int32)
    neighbours = draw_neighbours(jax.random.fold_in(splits[7], 71), 0)
    coupling = jnp.clip(jnp.exp(math.log(0.2) - 1.89712 * jax.random.uniform(splits[3], (NB, NCELLS), jnp.float32) ** level_of(splits[3], (NB, NCELLS), ((1, 512),), -0.2, 0.2)), 0.03, 0.2)
    stiffness = jnp.clip(jnp.exp(math.log(1.0) - 2.3025851 * jax.random.uniform(splits[4], (NCELLS,), jnp.float32) ** level_of(splits[4], (NCELLS,), ((0, 512),), -0.2, 0.2)), 0.1, 1.0)
    lame = jnp.clip(jnp.exp(math.log(0.5) - 2.3025851 * jax.random.uniform(splits[5], (NCELLS,), jnp.float32) ** level_of(splits[5], (NCELLS,), ((0, 512),), -0.2, 0.2)), 0.05, 0.5)
    load = centred(splits[6], (COMPONENTS, NODES, NODES, NODES, NCELLS), 1.0, 6.0, ((4, 512),), jnp.float32)
    return dict(degree=degree, curve_order=curve_order, neighbours=neighbours, coupling=coupling, stiffness=stiffness, lame=lame, load=load)


def mass_table():
    spots = jnp.arange(NODES)
    beside = jnp.abs(spots[:, None] - spots[None, :]) == 1
    return jnp.where(beside, 0.15, 0.0).astype(jnp.float32) + jnp.eye(NODES, dtype=jnp.float32)


def stiff_table():
    spots = jnp.arange(NODES)
    beside = jnp.abs(spots[:, None] - spots[None, :]) == 1
    return jnp.where(beside, -1.0, 0.0).astype(jnp.float32) + 2.0 * jnp.eye(NODES, dtype=jnp.float32)


def along(table, field, which):
    forms = {1: "ip,apjkc->aijkc", 2: "jp,aipkc->aijkc", 3: "kp,aijpc->aijkc"}
    return jnp.einsum(forms[which], table, field, precision=lax.Precision.HIGHEST)


def local_part(field, stiffness, lame):
    mass = mass_table()
    stiff = stiff_table()
    mixing = (jnp.ones((COMPONENTS, COMPONENTS), jnp.float32) + jnp.eye(COMPONENTS, dtype=jnp.float32)) * 0.5
    after_z = along(mass, field, 3)
    after_yz = along(mass, after_z, 2)
    term_x = along(stiff, after_yz, 1)
    full_mass = along(mass, after_yz, 1)
    term_y = along(stiff, along(mass, after_z, 1), 2)
    term_z = along(stiff, along(mass, along(mass, field, 2), 1), 3)
    mixed = jnp.einsum("ab,bijkc->aijkc", mixing, full_mass, precision=lax.Precision.HIGHEST)
    return stiffness * (term_x + term_y + term_z) + lame * mixed


def node_mask(cdeg):
    spots = jnp.arange(NODES, dtype=jnp.int32)
    first = (spots[:, None] <= cdeg[None, :])
    inside = first[:, None, None, :] & first[None, :, None, :] & first[None, None, :, :]
    return inside[None].astype(jnp.float32)


def reference(degree, curve_order, neighbours, coupling, stiffness, lame, load):
    devices = N_GROUP * N_RANK
    index = (jnp.arange(devices, dtype=jnp.int32)[:, None] * CELLS_DEV + curve_order).reshape(-1).astype(jnp.int32)
    cdeg = degree[index]
    rhs = load[..., index]
    weight = (cdeg + 1) ** 3
    inclusive = jnp.cumsum(weight).astype(jnp.int32)
    total = inclusive[-1]
    share = (total + devices - 1) // devices
    owner = ((inclusive - weight) // share).astype(jnp.int32)
    mask = node_mask(cdeg)
    inverse = mask / (6.0 * stiffness + lame)
    other = stiffness[neighbours]
    weights = coupling * (2.0 * stiffness[None, :] * other / (stiffness[None, :] + other))

    def operate(field):
        local = local_part(field, stiffness, lame)
        couple = jnp.zeros_like(field)
        for k in range(NB):
            couple = couple + weights[k] * field[..., neighbours[k]]
            couple = couple.at[..., neighbours[k]].add(weights[k] * field)
        return mask * (local - couple)

    theta = (5.0 + 0.5) / 2.0
    delta = (5.0 - 0.5) / 2.0
    sigma = theta / delta
    smoothed = jnp.zeros_like(rhs)
    for sweep in range(SWEEPS):
        rho_old = 1.0 / sigma
        if sweep == 0:
            resid = rhs
        else:
            resid = rhs - operate(smoothed)
        step = inverse * resid / theta
        smoothed = smoothed + step
        for inner in range(DEGREE - 1):
            rho = 1.0 / (2.0 * sigma - rho_old)
            resid = rhs - operate(smoothed)
            step = rho * rho_old * step + (2.0 * rho / delta) * inverse * resid
            smoothed = smoothed + step
            rho_old = rho
    return owner, smoothed
```

```python
import jax
import jax.numpy as jnp
from jax import lax
from jax.experimental import pallas as pl
from jax.experimental.pallas import tpu as pltpu
from jax.sharding import PartitionSpec as P

NODES = 6
COMPONENTS = 3
REACH = 32
SWEEPS = 2
DEGREE = 3
CELLS = 128
ROWS = COMPONENTS * NODES * NODES
QUADS = ROWS // 4
DENSE = 3 * QUADS
EDGE = 21
AXES = ("group", "rank")
THETA = (5.0 + 0.5) / 2.0
DELTA = (5.0 - 0.5) / 2.0
SIGMA = THETA / DELTA
F32, BF16, I32 = jnp.float32, jnp.bfloat16, jnp.int32


def iota(shape, dim):
    return lax.broadcasted_iota(I32, shape, dim)


def halves(x):
    high = x.astype(BF16)
    return high, (x - high.astype(F32)).astype(BF16)


def pack_kernel(load, order, degree, near, coupling, stiffness, lame, main, up, down, exclusive, padded):
    padded[:, NODES:8, :] = jnp.zeros((ROWS, 8 - NODES, CELLS), F32)
    padded[:, 0:NODES, :] = load[...]
    place = (iota((CELLS, CELLS), 0) == order[...]).astype(BF16)
    field = padded[...].reshape(ROWS * 8, CELLS)
    parts = jnp.concatenate(halves(field), axis=1)
    moved = jnp.dot(parts, jnp.concatenate([place, place], axis=0), preferred_element_type=F32)
    quads = moved.reshape(QUADS, 4, 8, CELLS)
    inner = iota((QUADS, 8, CELLS), 1) < NODES
    dense = [
        jnp.where(inner, quads[:, s], pltpu.roll(quads[:, 3], 6 - 2 * s, 1)) for s in range(3)
    ]
    degrees = jnp.broadcast_to(degree[...], (8, CELLS)).astype(F32).astype(BF16)
    cdeg = jnp.dot(degrees, place, preferred_element_type=F32)
    weight = (cdeg + 1.0) * (cdeg + 1.0) * (cdeg + 1.0)
    earlier = (iota((CELLS, CELLS), 0) < iota((CELLS, CELLS), 1)).astype(BF16)
    sums = jnp.dot(weight.astype(BF16), earlier, preferred_element_type=F32)
    exclusive[...] = sums[0:1].astype(I32)
    lane = iota((NB, CELLS), 1)
    offset = ((near[...] - lane + 64) & (CELLS - 1)) - 64
    rows = ((lane + offset) & (2 * CELLS - 1)).astype(F32)
    small0 = jnp.concatenate([rows, stiffness[...], lame[...]], axis=0)
    small1 = jnp.concatenate([coupling[...], cdeg[0:2]], axis=0)
    for s in range(3):
        main[s * QUADS : (s + 1) * QUADS] = dense[s]
    main[DENSE] = small0
    main[DENSE + 1] = small1
    lanes = iota((EDGE, 8, CELLS), 2)
    first, last = None, None
    for s in range(4):
        count = min(EDGE, DENSE - s * EDGE)
        piece = main[s * EDGE : s * EDGE + count]
        if count < EDGE:
            piece = jnp.concatenate([piece, jnp.zeros((EDGE - count, 8, CELLS), F32)], axis=0)
        head = piece if s == 0 else pltpu.roll(piece, REACH * s, 2)
        tail = piece if s == 3 else pltpu.roll(piece, REACH * s + REACH, 2)
        if s == 0:
            first, last = head, tail
        else:
            first = jnp.where(lanes >= REACH * s, head, first)
            last = jnp.where(lanes >= REACH * s, tail, last)
    down[0:EDGE] = first
    down[EDGE] = small0
    down[EDGE + 1] = small1
    up[0:EDGE] = last
    up[EDGE] = small0
    up[EDGE + 1] = small1


NB = 6
LEFT, OWN, RIGHT, OUTER, RIM = range(5)


def spread(dense):
    sub = iota((QUADS, 8, CELLS), 1)
    parts = [dense[s * QUADS : (s + 1) * QUADS] for s in range(3)]
    zero = jnp.zeros((QUADS, 8, CELLS), F32)
    tails = [pltpu.roll(parts[s], 2 * s + 2, 1) for s in range(3)]
    fourth = jnp.where(sub < 2, tails[0], jnp.where(sub < 4, tails[1], jnp.where(sub < 6, tails[2], zero)))
    return [jnp.where(sub < NODES, part, zero) for part in parts] + [fourth]


def smooth_kernel(own, left, right, outer_left, outer_right, out,
                  rhs, step, state_a, state_b, gain, stiff, table, low_table, couple, after_z, paired):
    low_lanes = lambda shape: iota(shape, len(shape) - 1) < 64

    for tile, source in ((LEFT, left), (OWN, own), (RIGHT, right)):
        for s, part in enumerate(spread(source[0:DENSE])):
            rhs[tile, :, s] = part
    pieces = []
    for s in range(4):
        lo = outer_right[0:EDGE] if s == 0 else pltpu.roll(outer_right[0:EDGE], CELLS - REACH * s, 2)
        hi = outer_left[0:EDGE] if s == 3 else pltpu.roll(outer_left[0:EDGE], 96 - REACH * s, 2)
        pieces.append(jnp.where(low_lanes((EDGE, 8, CELLS)), lo, hi))
    joined = jnp.concatenate(pieces, axis=0)
    for s, part in enumerate(spread(joined[0:DENSE])):
        rhs[OUTER, :, s] = part

    pick = low_lanes((8, CELLS))
    small = {
        LEFT: (left[DENSE], left[DENSE + 1]),
        OWN: (own[DENSE], own[DENSE + 1]),
        RIGHT: (right[DENSE], right[DENSE + 1]),
        OUTER: (
            jnp.where(pick, outer_right[EDGE], outer_left[EDGE]),
            jnp.where(pick, outer_right[EDGE + 1], outer_left[EDGE + 1]),
        ),
    }
    small[RIM] = tuple(jnp.where(pick, small[RIGHT][n], small[LEFT][n]) for n in range(2))
    sub = iota((8, CELLS), 0)
    for tile in range(5):
        shear, first_lame = small[tile][0][6:7], small[tile][0][7:8]
        diagonal = 1.0 / jnp.maximum(6.0 * shear + first_lame, 1e-6)
        cdeg = small[tile][1][6:7]
        for m in range(NODES):
            top = jnp.maximum(sub, m).astype(F32)
            gain[tile, m] = jnp.where(top <= cdeg, jnp.broadcast_to(diagonal, (8, CELLS)), 0.0)
        stiff[tile, 0] = jnp.broadcast_to(shear * (26.0 / 3.0), (8, CELLS))
        stiff[tile, 1] = jnp.broadcast_to(0.5 * first_lame - 20.0 * shear, (8, CELLS))
        stiff[tile, 2] = jnp.broadcast_to(0.5 * first_lame, (8, CELLS))

    def listed(tile, start, count):
        rows, weights = small[tile]
        place = (iota((count, CELLS), 0) + start).astype(F32)
        total = jnp.zeros((count, CELLS), F32)
        for k in range(NB):
            total = total + jnp.where(place == rows[k : k + 1], weights[k : k + 1], 0.0)
        return total

    inside = {tile: listed(tile, 0, CELLS) for tile in (LEFT, OWN, RIGHT)}
    across = {tile: listed(tile, CELLS, CELLS) for tile in (LEFT, OWN, RIGHT, OUTER)}
    wide = low_lanes((CELLS, CELLS))
    sides = {LEFT: (OWN, OUTER), OWN: (RIGHT, LEFT), RIGHT: (OUTER, OWN)}
    shear_of = {tile: jnp.broadcast_to(small[tile][0][6:7], (CELLS, CELLS)) for tile in range(4)}
    full = {}
    for tile, (after, before) in sides.items():
        top = inside[tile] + inside[tile].T
        bottom = across[tile] + jnp.where(wide, across[after], across[before]).T
        here = shear_of[tile]
        beside = jnp.where(wide, shear_of[after], shear_of[before])
        halved = []
        for values, other in ((top, here.T), (bottom, beside.T)):
            halved.append(values * (2.0 * here * other / jnp.maximum(here + other, 1e-6)))
        full[tile] = halved
    q = iota((CELLS, CELLS), 0)
    to_right = wide
    rim_top = jnp.where(
        to_right,
        jnp.where(q < 64, full[RIGHT][0], 0.0),
        jnp.where(q >= 64, full[LEFT][0], 0.0),
    )
    rim_bottom = jnp.where(
        to_right,
        jnp.where(q >= 96, full[RIGHT][1], jnp.where(q >= 64, full[RIGHT][0], 0.0)),
        jnp.where(q < 32, full[LEFT][1], jnp.where(q < 64, full[LEFT][0], 0.0)),
    )
    full[RIM] = [rim_top, rim_bottom]
    for slot, tile in enumerate((LEFT, OWN, RIGHT, RIM)):
        for half in range(2):
            high, low = halves(full[tile][half])
            table[slot, half * CELLS : (half + 1) * CELLS] = high
            table[slot, (2 + half) * CELLS : (3 + half) * CELLS] = high
            low_table[slot, half * CELLS : (half + 1) * CELLS] = low
    slot_of = {LEFT: 0, OWN: 1, RIGHT: 2, RIM: 3}

    edge = jnp.zeros((COMPONENTS, 6, 8, CELLS), F32)
    after_z[:, 0] = edge
    after_z[:, 7] = edge
    paired[:, 0] = edge
    paired[:, 7] = edge

    def first_step(tile):
        for r in range(QUADS):
            for s in range(4):
                row = 4 * r + s
                value = gain[tile, max(row // 6 % 6, row % 6)] * rhs[tile, r, s] * (1.0 / THETA)
                step[tile, r, s] = value
                state_a[tile, r, s] = value

    for tile in (LEFT, OWN, RIGHT, OUTER):
        first_step(tile)

    def apply(tile, source, beside, target, keep, scale, final=None):
        slot = slot_of[tile]
        here = source[tile].reshape(ROWS * 8, CELLS)
        there = beside().reshape(ROWS * 8, CELLS)
        (h1, l1), (h2, l2) = halves(here), halves(there)
        left_hand = jnp.concatenate([h1, h2, l1, l2], axis=1)
        result = jnp.dot(left_hand, table[slot], preferred_element_type=F32)
        result = result + jnp.dot(left_hand[:, : 2 * CELLS], low_table[slot], preferred_element_type=F32)
        couple[...] = result.reshape(COMPONENTS, 6, 6, 8, CELLS)
        for a in range(COMPONENTS):
            for i in range(6):
                u, y = [], []
                for j in range(6):
                    row = (a * 6 + i) * 6 + j
                    value = source[tile, row // 4, row % 4]
                    u.append(value)
                    y.append(value + 0.15 * (pltpu.roll(value, 1, 0) + pltpu.roll(value, 7, 0)))
                for j in range(6):
                    def beside_sum(values):
                        if j == 0:
                            return values[1]
                        if j == 5:
                            return values[4]
                        return values[j - 1] + values[j + 1]
                    z = y[j] + 0.15 * beside_sum(y)
                    x2 = u[j] + 0.15 * beside_sum(u)
                    after_z[a, i + 1, j] = z
                    paired[a, i + 1, j] = y[j] + x2
        k0, k1, k2 = stiff[tile, 0], stiff[tile, 1], stiff[tile, 2]
        for i in range(6):
            for j in range(6):
                ms, vs = [], []
                for a in range(COMPONENTS):
                    z = after_z[a, i + 1, j]
                    ms.append(z + 0.15 * (after_z[a, i, j] + after_z[a, i + 2, j]))
                    vs.append(z + paired[a, i + 1, j] + 0.15 * (paired[a, i, j] + paired[a, i + 2, j]))
                mixed = k2 * (ms[0] + ms[1] + ms[2])
                g = gain[tile, max(i, j)] * scale
                for a in range(COMPONENTS):
                    row = (a * 6 + i) * 6 + j
                    r, s = row // 4, row % 4
                    resid = (rhs[tile, r, s] - mixed) + (couple[a, i, j] - k0 * vs[a] - k1 * ms[a])
                    delta = g * resid
                    if keep is not None:
                        delta = delta + keep * step[tile, r, s]
                    value = source[tile, r, s] + delta
                    if final is None:
                        step[tile, r, s] = delta
                        target[tile, r, s] = value
                    else:
                        final[row] = value[0:NODES]

    rho0 = 1.0 / SIGMA
    rho1 = 1.0 / (2.0 * SIGMA - rho0)
    rho2 = 1.0 / (2.0 * SIGMA - rho1)
    first = (rho1 * rho0, 2.0 * rho1 / DELTA)
    second = (rho2 * rho1, 2.0 * rho2 / DELTA)
    low = low_lanes((QUADS, 4, 8, CELLS))
    join = lambda x, y: jnp.where(low, x, y)

    for source, target, (keep, scale) in ((state_a, state_b, first), (state_b, state_a, second)):
        apply(LEFT, source, lambda: join(source[OWN], state_a[OUTER]), target, keep, scale)
        apply(OWN, source, lambda: join(source[RIGHT], source[LEFT]), target, keep, scale)
        apply(RIGHT, source, lambda: join(state_a[OUTER], source[OWN]), target, keep, scale)
    state_a[RIM] = join(state_a[RIGHT], state_a[LEFT])
    rhs[RIM] = join(rhs[RIGHT], rhs[LEFT])
    lanes = iota((QUADS, 4, 8, CELLS), 3)
    ends = (lanes < 32) | (lanes >= 96)
    for source, target, (keep, scale) in (
        (state_a, state_b, (None, 1.0 / THETA)),
        (state_b, state_a, first),
    ):
        apply(OWN, source, lambda: source[RIM], target, keep, scale)
        apply(RIM, source, lambda: jnp.where(ends, source[OWN], join(state_a[LEFT], state_a[RIGHT])), target, keep, scale)
    apply(OWN, state_a, lambda: state_a[RIM], None, second[0], second[1], out)


def shards(degree, curve_order, neighbours, coupling, stiffness, lame, load):
    devices = lax.axis_size(AXES)
    groups, ranks = lax.axis_size("group"), lax.axis_size("rank")
    group, rank = lax.axis_index("group"), lax.axis_index("rank")
    vmem = pl.BlockSpec(memory_space=pltpu.VMEM)
    row = lambda x: x.reshape(1, CELLS)
    packed = pl.pallas_call(
        pack_kernel,
        out_shape=(
            jax.ShapeDtypeStruct((DENSE + 2, 8, CELLS), F32),
            jax.ShapeDtypeStruct((EDGE + 2, 8, CELLS), F32),
            jax.ShapeDtypeStruct((EDGE + 2, 8, CELLS), F32),
            jax.ShapeDtypeStruct((1, CELLS), I32),
        ),
        in_specs=[vmem] * 7,
        out_specs=[vmem] * 4,
        scratch_shapes=[pltpu.VMEM((ROWS, 8, CELLS), F32)],
        compiler_params=pltpu.CompilerParams(vmem_limit_bytes=32 * 1024 * 1024),
        name="pack",
    )(load.reshape(ROWS, NODES, CELLS), curve_order, row(degree), neighbours, coupling, row(stiffness), row(lame))
    main, up, down, exclusive = packed

    def shifted(array, by):
        pairs = [(i, i + by) for i in range(max(0, -by), min(devices, devices - by))]
        return lax.ppermute(array, AXES, pairs)

    left, right = shifted(main, 1), shifted(main, -1)
    outer_left, outer_right = shifted(up, 2), shifted(down, -2)

    local_total = jnp.sum((degree + 1) ** 3)
    by_rank = jnp.where(jnp.arange(ranks, dtype=I32) == rank, local_total, 0)
    by_rank = lax.psum(by_rank, "rank")
    in_group = jnp.sum(jnp.where(jnp.arange(ranks, dtype=I32) < rank, by_rank, 0))
    by_group = jnp.where(jnp.arange(groups, dtype=I32) == group, jnp.sum(by_rank), 0)
    by_group = lax.psum(by_group, "group")
    before = in_group + jnp.sum(jnp.where(jnp.arange(groups, dtype=I32) < group, by_group, 0))
    share = (jnp.sum(by_group) + devices - 1) // devices
    owner = (before + exclusive.reshape(CELLS)) // share

    block = (QUADS, 4, 8, CELLS)
    smoothed = pl.pallas_call(
        smooth_kernel,
        out_shape=jax.ShapeDtypeStruct((ROWS, NODES, CELLS), F32),
        in_specs=[vmem] * 5,
        out_specs=vmem,
        scratch_shapes=[
            pltpu.VMEM((5, *block), F32),
            pltpu.VMEM((5, *block), F32),
            pltpu.VMEM((5, *block), F32),
            pltpu.VMEM((5, *block), F32),
            pltpu.VMEM((5, NODES, 8, CELLS), F32),
            pltpu.VMEM((5, 3, 8, CELLS), F32),
            pltpu.VMEM((4, 4 * CELLS, CELLS), BF16),
            pltpu.VMEM((4, 2 * CELLS, CELLS), BF16),
            pltpu.VMEM((COMPONENTS, 6, 6, 8, CELLS), F32),
            pltpu.VMEM((COMPONENTS, 8, 6, 8, CELLS), F32),
            pltpu.VMEM((COMPONENTS, 8, 6, 8, CELLS), F32),
        ],
        compiler_params=pltpu.CompilerParams(vmem_limit_bytes=48 * 1024 * 1024),
        name="smooth",
    )(main, left, right, outer_left, outer_right)
    return owner, smoothed.reshape(COMPONENTS, NODES, NODES, NODES, CELLS)


def solution(mesh):
    return jax.shard_map(
        shards,
        mesh=mesh,
        in_specs=(
            P(AXES),
            P(AXES, None),
            P(None, AXES),
            P(None, AXES),
            P(AXES),
            P(AXES),
            P(None, None, None, None, AXES),
        ),
        out_specs=(P(AXES), P(None, None, None, None, AXES)),
        check_vma=False,
    )
```

```python
import jax
import jax.numpy as jnp
from jax import lax
from jax.experimental import pallas as pl
from jax.experimental.pallas import tpu as pltpu
from jax.sharding import PartitionSpec as P

NODES = 6
COMPONENTS = 3
REACH = 32
SWEEPS = 2
DEGREE = 3
CELLS = 128
ROWS = COMPONENTS * NODES * NODES
QUADS = ROWS // 4
DENSE = 3 * QUADS
EDGE = 21
AXES = ("group", "rank")
THETA = (5.0 + 0.5) / 2.0
DELTA = (5.0 - 0.5) / 2.0
SIGMA = THETA / DELTA
F32, BF16, I32 = jnp.float32, jnp.bfloat16, jnp.int32


def iota(shape, dim):
    return lax.broadcasted_iota(I32, shape, dim)


def halves(x):
    high = x.astype(BF16)
    return high, (x - high.astype(F32)).astype(BF16)


def pack_kernel(*refs):
    sources, (main, up, down, exclusive, weights, padded), held, arrived = refs[:7], refs[7:13], refs[13:20], refs[20]
    copies = [pltpu.make_async_copy(a, b, arrived.at[n]) for n, (a, b) in enumerate(zip(sources, held))]
    for copy in copies:
        copy.start()
    padded[:, NODES:8, :] = jnp.zeros((ROWS, 8 - NODES, CELLS), F32)
    for copy in copies:
        copy.wait()
    load, order, degree, near, coupling, stiffness, lame = held
    padded[:, 0:NODES, :] = load[...]
    place = (iota((CELLS, CELLS), 0) == order[...]).astype(BF16)
    field = padded[...].reshape(ROWS * 8, CELLS)
    parts = jnp.concatenate(halves(field), axis=1)
    moved = jnp.dot(parts, jnp.concatenate([place, place], axis=0), preferred_element_type=F32)
    quads = moved.reshape(QUADS, 4, 8, CELLS)
    inner = iota((QUADS, 8, CELLS), 1) < NODES
    dense = [
        jnp.where(inner, quads[:, s], pltpu.roll(quads[:, 3], 6 - 2 * s, 1)) for s in range(3)
    ]
    degrees = jnp.broadcast_to(degree[...], (8, CELLS)).astype(F32).astype(BF16)
    cdeg = jnp.dot(degrees, place, preferred_element_type=F32)
    weight = (cdeg + 1.0) * (cdeg + 1.0) * (cdeg + 1.0)
    earlier = (iota((CELLS, CELLS), 0) < iota((CELLS, CELLS), 1)).astype(BF16)
    sums = jnp.dot(weight.astype(BF16), earlier, preferred_element_type=F32)
    exclusive[...] = sums[0:1].astype(I32)
    group = lax.axis_index("group")
    segment = jnp.sum(weight[0:1], axis=1, keepdims=True).astype(I32)
    weights[...] = jnp.where(iota((1, CELLS), 1) == group, segment, 0)
    lane = iota((NB, CELLS), 1)
    offset = ((near[...] - lane + 64) & (CELLS - 1)) - 64
    rows = ((lane + offset) & (2 * CELLS - 1)).astype(F32)
    small0 = jnp.concatenate([rows, stiffness[...], lame[...]], axis=0)
    small1 = jnp.concatenate([coupling[...], cdeg[0:2]], axis=0)
    for s in range(3):
        main[s * QUADS : (s + 1) * QUADS] = dense[s]
    main[DENSE] = small0
    main[DENSE + 1] = small1
    lanes = iota((EDGE, 8, CELLS), 2)
    first, last = None, None
    for s in range(4):
        count = min(EDGE, DENSE - s * EDGE)
        piece = main[s * EDGE : s * EDGE + count]
        if count < EDGE:
            piece = jnp.concatenate([piece, jnp.zeros((EDGE - count, 8, CELLS), F32)], axis=0)
        head = piece if s == 0 else pltpu.roll(piece, REACH * s, 2)
        tail = piece if s == 3 else pltpu.roll(piece, REACH * s + REACH, 2)
        if s == 0:
            first, last = head, tail
        else:
            first = jnp.where(lanes >= REACH * s, head, first)
            last = jnp.where(lanes >= REACH * s, tail, last)
    down[0:EDGE] = first
    down[EDGE] = small0
    down[EDGE + 1] = small1
    up[0:EDGE] = last
    up[EDGE] = small0
    up[EDGE + 1] = small1


NB = 6
LEFT, OWN, RIGHT, OUTER, RIM = range(5)


def spread(dense):
    sub = iota((QUADS, 8, CELLS), 1)
    parts = [dense[s * QUADS : (s + 1) * QUADS] for s in range(3)]
    zero = jnp.zeros((QUADS, 8, CELLS), F32)
    tails = [pltpu.roll(parts[s], 2 * s + 2, 1) for s in range(3)]
    fourth = jnp.where(sub < 2, tails[0], jnp.where(sub < 4, tails[1], jnp.where(sub < 6, tails[2], zero)))
    return [jnp.where(sub < NODES, part, zero) for part in parts] + [fourth]


def smooth_kernel(own, left, right, outer_left, outer_right, out,
                  rhs, step, state_a, state_b, gain, stiff, table, low_table, couple, after_z, paired):
    low_lanes = lambda shape: iota(shape, len(shape) - 1) < 64

    for tile, source in ((LEFT, left), (OWN, own), (RIGHT, right)):
        for s, part in enumerate(spread(source[0:DENSE])):
            rhs[tile, :, s] = part
    pieces = []
    for s in range(4):
        lo = outer_right[0:EDGE] if s == 0 else pltpu.roll(outer_right[0:EDGE], CELLS - REACH * s, 2)
        hi = outer_left[0:EDGE] if s == 3 else pltpu.roll(outer_left[0:EDGE], 96 - REACH * s, 2)
        pieces.append(jnp.where(low_lanes((EDGE, 8, CELLS)), lo, hi))
    joined = jnp.concatenate(pieces, axis=0)
    for s, part in enumerate(spread(joined[0:DENSE])):
        rhs[OUTER, :, s] = part

    pick = low_lanes((8, CELLS))
    small = {
        LEFT: (left[DENSE], left[DENSE + 1]),
        OWN: (own[DENSE], own[DENSE + 1]),
        RIGHT: (right[DENSE], right[DENSE + 1]),
        OUTER: (
            jnp.where(pick, outer_right[EDGE], outer_left[EDGE]),
            jnp.where(pick, outer_right[EDGE + 1], outer_left[EDGE + 1]),
        ),
    }
    small[RIM] = tuple(jnp.where(pick, small[RIGHT][n], small[LEFT][n]) for n in range(2))
    sub = iota((8, CELLS), 0)
    for tile in range(5):
        shear, first_lame = small[tile][0][6:7], small[tile][0][7:8]
        diagonal = 1.0 / jnp.maximum(6.0 * shear + first_lame, 1e-6)
        cdeg = small[tile][1][6:7]
        for m in range(NODES):
            top = jnp.maximum(sub, m).astype(F32)
            gain[tile, m] = jnp.where(top <= cdeg, jnp.broadcast_to(diagonal, (8, CELLS)), 0.0)
        stiff[tile, 0] = jnp.broadcast_to(shear * (26.0 / 3.0), (8, CELLS))
        stiff[tile, 1] = jnp.broadcast_to(0.5 * first_lame - 20.0 * shear, (8, CELLS))
        stiff[tile, 2] = jnp.broadcast_to(0.5 * first_lame, (8, CELLS))

    def listed(tile, start, count):
        rows, weights = small[tile]
        place = (iota((count, CELLS), 0) + start).astype(F32)
        total = jnp.zeros((count, CELLS), F32)
        for k in range(NB):
            total = total + jnp.where(place == rows[k : k + 1], weights[k : k + 1], 0.0)
        return total

    inside = {tile: listed(tile, 0, CELLS) for tile in (LEFT, OWN, RIGHT)}
    across = {tile: listed(tile, CELLS, CELLS) for tile in (LEFT, OWN, RIGHT, OUTER)}
    wide = low_lanes((CELLS, CELLS))
    sides = {LEFT: (OWN, OUTER), OWN: (RIGHT, LEFT), RIGHT: (OUTER, OWN)}
    shear_of = {tile: jnp.broadcast_to(small[tile][0][6:7], (CELLS, CELLS)) for tile in range(4)}
    full = {}
    for tile, (after, before) in sides.items():
        top = inside[tile] + inside[tile].T
        bottom = across[tile] + jnp.where(wide, across[after], across[before]).T
        here = shear_of[tile]
        beside = jnp.where(wide, shear_of[after], shear_of[before])
        halved = []
        for values, other in ((top, here.T), (bottom, beside.T)):
            halved.append(values * (2.0 * here * other / jnp.maximum(here + other, 1e-6)))
        full[tile] = halved
    q = iota((CELLS, CELLS), 0)
    to_right = wide
    rim_top = jnp.where(
        to_right,
        jnp.where(q < 64, full[RIGHT][0], 0.0),
        jnp.where(q >= 64, full[LEFT][0], 0.0),
    )
    rim_bottom = jnp.where(
        to_right,
        jnp.where(q >= 96, full[RIGHT][1], jnp.where(q >= 64, full[RIGHT][0], 0.0)),
        jnp.where(q < 32, full[LEFT][1], jnp.where(q < 64, full[LEFT][0], 0.0)),
    )
    full[RIM] = [rim_top, rim_bottom]
    for slot, tile in enumerate((LEFT, OWN, RIGHT, RIM)):
        for half in range(2):
            high, low = halves(full[tile][half])
            table[slot, half * CELLS : (half + 1) * CELLS] = high
            table[slot, (2 + half) * CELLS : (3 + half) * CELLS] = high
            low_table[slot, half * CELLS : (half + 1) * CELLS] = low
    slot_of = {LEFT: 0, OWN: 1, RIGHT: 2, RIM: 3}

    edge = jnp.zeros((COMPONENTS, 6, 8, CELLS), F32)
    after_z[:, 0] = edge
    after_z[:, 7] = edge
    paired[:, 0] = edge
    paired[:, 7] = edge

    def first_step(tile):
        for r in range(QUADS):
            for s in range(4):
                row = 4 * r + s
                value = gain[tile, max(row // 6 % 6, row % 6)] * rhs[tile, r, s] * (1.0 / THETA)
                step[tile, r, s] = value
                state_a[tile, r, s] = value

    for tile in (LEFT, OWN, RIGHT, OUTER):
        first_step(tile)

    def apply(tile, source, beside, target, keep, scale, final=None):
        slot = slot_of[tile]
        here = source[tile].reshape(ROWS * 8, CELLS)
        there = beside().reshape(ROWS * 8, CELLS)
        (h1, l1), (h2, l2) = halves(here), halves(there)
        left_hand = jnp.concatenate([h1, h2, l1, l2], axis=1)
        result = jnp.dot(left_hand, table[slot], preferred_element_type=F32)
        result = result + jnp.dot(left_hand[:, : 2 * CELLS], low_table[slot], preferred_element_type=F32)
        couple[...] = result.reshape(COMPONENTS, 6, 6, 8, CELLS)
        for a in range(COMPONENTS):
            for i in range(6):
                u, y = [], []
                for j in range(6):
                    row = (a * 6 + i) * 6 + j
                    value = source[tile, row // 4, row % 4]
                    u.append(value)
                    y.append(value + 0.15 * (pltpu.roll(value, 1, 0) + pltpu.roll(value, 7, 0)))
                for j in range(6):
                    def beside_sum(values):
                        if j == 0:
                            return values[1]
                        if j == 5:
                            return values[4]
                        return values[j - 1] + values[j + 1]
                    z = y[j] + 0.15 * beside_sum(y)
                    x2 = u[j] + 0.15 * beside_sum(u)
                    after_z[a, i + 1, j] = z
                    paired[a, i + 1, j] = y[j] + x2
        k0, k1, k2 = stiff[tile, 0], stiff[tile, 1], stiff[tile, 2]
        for i in range(6):
            for j in range(6):
                ms, vs = [], []
                for a in range(COMPONENTS):
                    z = after_z[a, i + 1, j]
                    ms.append(z + 0.15 * (after_z[a, i, j] + after_z[a, i + 2, j]))
                    vs.append(z + paired[a, i + 1, j] + 0.15 * (paired[a, i, j] + paired[a, i + 2, j]))
                mixed = k2 * (ms[0] + ms[1] + ms[2])
                g = gain[tile, max(i, j)] * scale
                for a in range(COMPONENTS):
                    row = (a * 6 + i) * 6 + j
                    r, s = row // 4, row % 4
                    resid = (rhs[tile, r, s] - mixed) + (couple[a, i, j] - k0 * vs[a] - k1 * ms[a])
                    delta = g * resid
                    if keep is not None:
                        delta = delta + keep * step[tile, r, s]
                    value = source[tile, r, s] + delta
                    if final is None:
                        step[tile, r, s] = delta
                        target[tile, r, s] = value
                    else:
                        final[row] = value[0:NODES]

    rho0 = 1.0 / SIGMA
    rho1 = 1.0 / (2.0 * SIGMA - rho0)
    rho2 = 1.0 / (2.0 * SIGMA - rho1)
    first = (rho1 * rho0, 2.0 * rho1 / DELTA)
    second = (rho2 * rho1, 2.0 * rho2 / DELTA)
    low = low_lanes((QUADS, 4, 8, CELLS))
    join = lambda x, y: jnp.where(low, x, y)

    for source, target, (keep, scale) in ((state_a, state_b, first), (state_b, state_a, second)):
        apply(LEFT, source, lambda: join(source[OWN], state_a[OUTER]), target, keep, scale)
        apply(OWN, source, lambda: join(source[RIGHT], source[LEFT]), target, keep, scale)
        apply(RIGHT, source, lambda: join(state_a[OUTER], source[OWN]), target, keep, scale)
    state_a[RIM] = join(state_a[RIGHT], state_a[LEFT])
    rhs[RIM] = join(rhs[RIGHT], rhs[LEFT])
    lanes = iota((QUADS, 4, 8, CELLS), 3)
    ends = (lanes < 32) | (lanes >= 96)
    for source, target, (keep, scale) in (
        (state_a, state_b, (None, 1.0 / THETA)),
        (state_b, state_a, first),
    ):
        apply(OWN, source, lambda: source[RIM], target, keep, scale)
        apply(RIM, source, lambda: jnp.where(ends, source[OWN], join(state_a[LEFT], state_a[RIGHT])), target, keep, scale)
    apply(OWN, state_a, lambda: state_a[RIM], None, second[0], second[1], out)


def owner_kernel(totals, exclusive, owner):
    group, rank = lax.axis_index("group"), lax.axis_index("rank")
    devices = lax.axis_size(AXES)
    values = totals[...].astype(F32)
    rows, columns = iota(values.shape, 0), iota(values.shape, 1)
    earlier = (columns < group) | ((columns == group) & (rows < rank))
    whole = lambda x: jnp.sum(jnp.sum(x, axis=0, keepdims=True), axis=1, keepdims=True)
    before = whole(jnp.where(earlier, values, 0.0)) + exclusive[...].astype(F32)
    share = jnp.floor((whole(values) + (devices - 1.0)) * (1.0 / devices))
    place = jnp.floor(before * (1.0 / share))
    left = before - place * share
    place = place + jnp.where(left < 0.0, -1.0, jnp.where(left >= share, 1.0, 0.0))
    owner[...] = place.astype(I32)


def shards(degree, curve_order, neighbours, coupling, stiffness, lame, load):
    devices = lax.axis_size(AXES)
    ranks = lax.axis_size("rank")
    vmem = pl.BlockSpec(memory_space=pltpu.VMEM)
    row = lambda x: x.reshape(1, CELLS)
    arguments = (load.reshape(ROWS, NODES, CELLS), curve_order, row(degree), neighbours, coupling, row(stiffness), row(lame))
    packed = pl.pallas_call(
        pack_kernel,
        out_shape=(
            jax.ShapeDtypeStruct((DENSE + 2, 8, CELLS), F32),
            jax.ShapeDtypeStruct((EDGE + 2, 8, CELLS), F32),
            jax.ShapeDtypeStruct((EDGE + 2, 8, CELLS), F32),
            jax.ShapeDtypeStruct((1, CELLS), I32),
            jax.ShapeDtypeStruct((1, CELLS), I32),
        ),
        in_specs=[pl.BlockSpec(memory_space=pltpu.HBM)] * 7,
        out_specs=[vmem] * 5,
        scratch_shapes=[
            pltpu.VMEM((ROWS, 8, CELLS), F32),
            *[pltpu.VMEM(x.shape, x.dtype) for x in arguments],
            pltpu.SemaphoreType.DMA((7,)),
        ],
        compiler_params=pltpu.CompilerParams(vmem_limit_bytes=32 * 1024 * 1024),
        name="pack",
    )(*arguments)
    main, up, down, exclusive, weights = packed
    weights = lax.psum(weights, "group")
    main, up, down, weights = lax.optimization_barrier((main, up, down, weights))

    def shifted(array, by):
        pairs = [(i, i + by) for i in range(max(0, -by), min(devices, devices - by))]
        return lax.ppermute(array, AXES, pairs)

    left, right = shifted(main, 1), shifted(main, -1)
    outer_left, outer_right = shifted(up, 2), shifted(down, -2)

    totals = lax.all_to_all(jnp.broadcast_to(weights, (ranks, CELLS)), "rank", 0, 0, tiled=True)

    block = (QUADS, 4, 8, CELLS)
    smoothed = pl.pallas_call(
        smooth_kernel,
        out_shape=jax.ShapeDtypeStruct((ROWS, NODES, CELLS), F32),
        in_specs=[vmem] * 5,
        out_specs=vmem,
        cost_estimate=pl.CostEstimate(flops=7 * 10**9, bytes_accessed=10**6, transcendentals=0),
        scratch_shapes=[
            pltpu.VMEM((5, *block), F32),
            pltpu.VMEM((5, *block), F32),
            pltpu.VMEM((5, *block), F32),
            pltpu.VMEM((5, *block), F32),
            pltpu.VMEM((5, NODES, 8, CELLS), F32),
            pltpu.VMEM((5, 3, 8, CELLS), F32),
            pltpu.VMEM((4, 4 * CELLS, CELLS), BF16),
            pltpu.VMEM((4, 2 * CELLS, CELLS), BF16),
            pltpu.VMEM((COMPONENTS, 6, 6, 8, CELLS), F32),
            pltpu.VMEM((COMPONENTS, 8, 6, 8, CELLS), F32),
            pltpu.VMEM((COMPONENTS, 8, 6, 8, CELLS), F32),
        ],
        compiler_params=pltpu.CompilerParams(vmem_limit_bytes=48 * 1024 * 1024),
        name="smooth",
    )(main, left, right, outer_left, outer_right)
    totals, smoothed = lax.optimization_barrier((totals, smoothed))
    owner = pl.pallas_call(
        owner_kernel,
        out_shape=jax.ShapeDtypeStruct((1, CELLS), I32),
        in_specs=[pl.BlockSpec(), vmem],
        out_specs=vmem,
        name="owner",
    )(totals.reshape(ranks, CELLS), exclusive)
    return owner.reshape(CELLS), smoothed.reshape(COMPONENTS, NODES, NODES, NODES, CELLS)


def solution(mesh):
    return jax.shard_map(
        shards,
        mesh=mesh,
        in_specs=(
            P(AXES),
            P(AXES, None),
            P(None, AXES),
            P(None, AXES),
            P(AXES),
            P(AXES),
            P(None, None, None, None, AXES),
        ),
        out_specs=(P(AXES), P(None, None, None, None, AXES)),
        check_vma=False,
    )
```

```python
import jax
import jax.numpy as jnp
from jax import lax
from jax.experimental import pallas as pl
from jax.experimental.pallas import tpu as pltpu
from jax.sharding import PartitionSpec as P

NODES = 6
COMPONENTS = 3
REACH = 32
SWEEPS = 2
DEGREE = 3
CELLS = 128
ROWS = COMPONENTS * NODES * NODES
QUADS = ROWS // 4
DENSE = 3 * QUADS
EDGE = 21
AXES = ("group", "rank")
THETA = (5.0 + 0.5) / 2.0
DELTA = (5.0 - 0.5) / 2.0
SIGMA = THETA / DELTA
F32, BF16, I32 = jnp.float32, jnp.bfloat16, jnp.int32


def iota(shape, dim):
    return lax.broadcasted_iota(I32, shape, dim)


def halves(x):
    high = x.astype(BF16)
    return high, (x - high.astype(F32)).astype(BF16)


def pack_kernel(*refs):
    sources, (main, up, down, exclusive, weights, padded), held, arrived = refs[:7], refs[7:13], refs[13:20], refs[20]
    copies = [pltpu.make_async_copy(a, b, arrived.at[n]) for n, (a, b) in enumerate(zip(sources, held))]
    for copy in copies:
        copy.start()
    padded[:, NODES:8, :] = jnp.zeros((ROWS, 8 - NODES, CELLS), F32)
    for copy in copies:
        copy.wait()
    load, order, degree, near, coupling, stiffness, lame = held
    padded[:, 0:NODES, :] = load[...]
    place = (iota((CELLS, CELLS), 0) == order[...]).astype(BF16)
    field = padded[...].reshape(ROWS * 8, CELLS)
    parts = jnp.concatenate(halves(field), axis=1)
    moved = jnp.dot(parts, jnp.concatenate([place, place], axis=0), preferred_element_type=F32)
    quads = moved.reshape(QUADS, 4, 8, CELLS)
    inner = iota((QUADS, 8, CELLS), 1) < NODES
    dense = [
        jnp.where(inner, quads[:, s], pltpu.roll(quads[:, 3], 6 - 2 * s, 1)) for s in range(3)
    ]
    degrees = jnp.broadcast_to(degree[...], (8, CELLS)).astype(F32).astype(BF16)
    cdeg = jnp.dot(degrees, place, preferred_element_type=F32)
    weight = (cdeg + 1.0) * (cdeg + 1.0) * (cdeg + 1.0)
    earlier = (iota((CELLS, CELLS), 0) < iota((CELLS, CELLS), 1)).astype(BF16)
    sums = jnp.dot(weight.astype(BF16), earlier, preferred_element_type=F32)
    exclusive[...] = sums[0:1].astype(I32)
    group = lax.axis_index("group")
    segment = jnp.sum(weight[0:1], axis=1, keepdims=True).astype(I32)
    weights[...] = jnp.where(iota((1, CELLS), 1) == group, segment, 0)
    lane = iota((NB, CELLS), 1)
    offset = ((near[...] - lane + 64) & (CELLS - 1)) - 64
    rows = ((lane + offset) & (2 * CELLS - 1)).astype(F32)
    small0 = jnp.concatenate([rows, stiffness[...], lame[...]], axis=0)
    small1 = jnp.concatenate([coupling[...], cdeg[0:2]], axis=0)
    for s in range(3):
        main[s * QUADS : (s + 1) * QUADS] = dense[s]
    main[DENSE] = small0
    main[DENSE + 1] = small1
    lanes = iota((EDGE, 8, CELLS), 2)
    first, last = None, None
    for s in range(4):
        count = min(EDGE, DENSE - s * EDGE)
        piece = main[s * EDGE : s * EDGE + count]
        if count < EDGE:
            piece = jnp.concatenate([piece, jnp.zeros((EDGE - count, 8, CELLS), F32)], axis=0)
        head = piece if s == 0 else pltpu.roll(piece, REACH * s, 2)
        tail = piece if s == 3 else pltpu.roll(piece, REACH * s + REACH, 2)
        if s == 0:
            first, last = head, tail
        else:
            first = jnp.where(lanes >= REACH * s, head, first)
            last = jnp.where(lanes >= REACH * s, tail, last)
    down[0:EDGE] = first
    down[EDGE] = small0
    down[EDGE + 1] = small1
    up[0:EDGE] = last
    up[EDGE] = small0
    up[EDGE + 1] = small1


NB = 6
LEFT, OWN, RIGHT, OUTER, RIM = range(5)


def spread(dense):
    sub = iota((QUADS, 8, CELLS), 1)
    parts = [dense[s * QUADS : (s + 1) * QUADS] for s in range(3)]
    zero = jnp.zeros((QUADS, 8, CELLS), F32)
    tails = [pltpu.roll(parts[s], 2 * s + 2, 1) for s in range(3)]
    fourth = jnp.where(sub < 2, tails[0], jnp.where(sub < 4, tails[1], jnp.where(sub < 6, tails[2], zero)))
    return [jnp.where(sub < NODES, part, zero) for part in parts] + [fourth]


def smooth_kernel(own, left, right, outer_left, outer_right, out,
                  results, sent, rhs, step, state_a, state_b, gain, stiff, table, couple, after_z, paired):
    low_lanes = lambda shape: iota(shape, len(shape) - 1) < 64

    for tile, source in ((LEFT, left), (OWN, own), (RIGHT, right)):
        for s, part in enumerate(spread(source[0:DENSE])):
            rhs[tile, :, s] = part
    pieces = []
    for s in range(4):
        lo = outer_right[0:EDGE] if s == 0 else pltpu.roll(outer_right[0:EDGE], CELLS - REACH * s, 2)
        hi = outer_left[0:EDGE] if s == 3 else pltpu.roll(outer_left[0:EDGE], 96 - REACH * s, 2)
        pieces.append(jnp.where(low_lanes((EDGE, 8, CELLS)), lo, hi))
    joined = jnp.concatenate(pieces, axis=0)
    for s, part in enumerate(spread(joined[0:DENSE])):
        rhs[OUTER, :, s] = part

    pick = low_lanes((8, CELLS))
    small = {
        LEFT: (left[DENSE], left[DENSE + 1]),
        OWN: (own[DENSE], own[DENSE + 1]),
        RIGHT: (right[DENSE], right[DENSE + 1]),
        OUTER: (
            jnp.where(pick, outer_right[EDGE], outer_left[EDGE]),
            jnp.where(pick, outer_right[EDGE + 1], outer_left[EDGE + 1]),
        ),
    }
    small[RIM] = tuple(jnp.where(pick, small[RIGHT][n], small[LEFT][n]) for n in range(2))
    sub = iota((8, CELLS), 0)
    for tile in range(5):
        shear, first_lame = small[tile][0][6:7], small[tile][0][7:8]
        diagonal = 1.0 / jnp.maximum(6.0 * shear + first_lame, 1e-6)
        cdeg = small[tile][1][6:7]
        for m in range(NODES):
            top = jnp.maximum(sub, m).astype(F32)
            gain[tile, m] = jnp.where(top <= cdeg, jnp.broadcast_to(diagonal, (8, CELLS)), 0.0)
        stiff[tile, 0] = jnp.broadcast_to(shear * (26.0 / 3.0), (8, CELLS))
        stiff[tile, 1] = jnp.broadcast_to(0.5 * first_lame - 20.0 * shear, (8, CELLS))
        stiff[tile, 2] = jnp.broadcast_to(0.5 * first_lame, (8, CELLS))

    def listed(tile, start, count):
        rows, weights = small[tile]
        place = (iota((count, CELLS), 0) + start).astype(F32)
        total = jnp.zeros((count, CELLS), F32)
        for k in range(NB):
            total = total + jnp.where(place == rows[k : k + 1], weights[k : k + 1], 0.0)
        return total

    inside = {tile: listed(tile, 0, CELLS) for tile in (LEFT, OWN, RIGHT)}
    across = {tile: listed(tile, CELLS, CELLS) for tile in (LEFT, OWN, RIGHT, OUTER)}
    wide = low_lanes((CELLS, CELLS))
    sides = {LEFT: (OWN, OUTER), OWN: (RIGHT, LEFT), RIGHT: (OUTER, OWN)}
    shear_of = {tile: jnp.broadcast_to(small[tile][0][6:7], (CELLS, CELLS)) for tile in range(4)}
    full = {}
    for tile, (after, before) in sides.items():
        top = inside[tile] + inside[tile].T
        bottom = across[tile] + jnp.where(wide, across[after], across[before]).T
        here = shear_of[tile]
        beside = jnp.where(wide, shear_of[after], shear_of[before])
        halved = []
        for values, other in ((top, here.T), (bottom, beside.T)):
            halved.append(values * (2.0 * here * other / jnp.maximum(here + other, 1e-6)))
        full[tile] = halved
    q = iota((CELLS, CELLS), 0)
    to_right = wide
    rim_top = jnp.where(
        to_right,
        jnp.where(q < 64, full[RIGHT][0], 0.0),
        jnp.where(q >= 64, full[LEFT][0], 0.0),
    )
    rim_bottom = jnp.where(
        to_right,
        jnp.where(q >= 96, full[RIGHT][1], jnp.where(q >= 64, full[RIGHT][0], 0.0)),
        jnp.where(q < 32, full[LEFT][1], jnp.where(q < 64, full[LEFT][0], 0.0)),
    )
    full[RIM] = [rim_top, rim_bottom]
    for slot, tile in enumerate((LEFT, OWN, RIGHT, RIM)):
        for half in range(2):
            high, low = halves(full[tile][half])
            table[slot, half * CELLS : (half + 1) * CELLS] = high
            table[slot, (2 + half) * CELLS : (3 + half) * CELLS] = high
            table[slot, (4 + half) * CELLS : (5 + half) * CELLS] = low
    slot_of = {LEFT: 0, OWN: 1, RIGHT: 2, RIM: 3}

    edge = jnp.zeros((COMPONENTS, 6, 8, CELLS), F32)
    after_z[:, 0] = edge
    after_z[:, 7] = edge
    paired[:, 0] = edge
    paired[:, 7] = edge

    def first_step(tile):
        for r in range(QUADS):
            for s in range(4):
                row = 4 * r + s
                value = gain[tile, max(row // 6 % 6, row % 6)] * rhs[tile, r, s] * (1.0 / THETA)
                step[tile, r, s] = value
                state_a[tile, r, s] = value

    for tile in (LEFT, OWN, RIGHT, OUTER):
        first_step(tile)

    def apply(tile, source, beside, target, keep, scale, final=None):
        slot = slot_of[tile]
        part = ROWS // 4 // COMPONENTS
        for a in range(COMPONENTS):
            here = source[tile, a * part : (a + 1) * part].reshape(part * 32, CELLS)
            there = beside(slice(a * part, (a + 1) * part)).reshape(part * 32, CELLS)
            (h1, l1), (h2, l2) = halves(here), halves(there)
            left_hand = jnp.concatenate([h1, h2, l1, l2, h1, h2], axis=1)
            result = jnp.dot(left_hand, table[slot], preferred_element_type=F32)
            couple[a] = result.reshape(6, 6, 8, CELLS)
            for i in range(6):
                u, y = [], []
                for j in range(6):
                    row = (a * 6 + i) * 6 + j
                    value = source[tile, row // 4, row % 4]
                    u.append(value)
                    y.append(value + 0.15 * (pltpu.roll(value, 1, 0) + pltpu.roll(value, 7, 0)))
                for j in range(6):
                    def beside_sum(values):
                        if j == 0:
                            return values[1]
                        if j == 5:
                            return values[4]
                        return values[j - 1] + values[j + 1]
                    z = y[j] + 0.15 * beside_sum(y)
                    x2 = u[j] + 0.15 * beside_sum(u)
                    after_z[a, i + 1, j] = z
                    paired[a, i + 1, j] = y[j] + x2
        k0, k1, k2 = stiff[tile, 0], stiff[tile, 1], stiff[tile, 2]
        for i in range(6):
            for j in range(6):
                ms, vs = [], []
                for a in range(COMPONENTS):
                    z = after_z[a, i + 1, j]
                    ms.append(z + 0.15 * (after_z[a, i, j] + after_z[a, i + 2, j]))
                    vs.append(z + paired[a, i + 1, j] + 0.15 * (paired[a, i, j] + paired[a, i + 2, j]))
                mixed = k2 * (ms[0] + ms[1] + ms[2])
                g = gain[tile, max(i, j)] * scale
                for a in range(COMPONENTS):
                    row = (a * 6 + i) * 6 + j
                    r, s = row // 4, row % 4
                    resid = (rhs[tile, r, s] - mixed) + (couple[a, i, j] - k0 * vs[a] - k1 * ms[a])
                    delta = g * resid
                    if keep is not None:
                        delta = delta + keep * step[tile, r, s]
                    value = source[tile, r, s] + delta
                    if final is None:
                        step[tile, r, s] = delta
                        target[tile, r, s] = value
                    else:
                        results[row] = value[0:NODES]
            if final is not None:
                for a in range(COMPONENTS):
                    rows = pl.ds((a * 6 + i) * 6, 6)
                    pltpu.make_async_copy(results.at[rows], final.at[rows], sent.at[a * 6 + i]).start()
        if final is not None:
            for n in range(COMPONENTS * 6):
                rows = pl.ds(n * 6, 6)
                pltpu.make_async_copy(results.at[rows], final.at[rows], sent.at[n]).wait()

    rho0 = 1.0 / SIGMA
    rho1 = 1.0 / (2.0 * SIGMA - rho0)
    rho2 = 1.0 / (2.0 * SIGMA - rho1)
    first = (rho1 * rho0, 2.0 * rho1 / DELTA)
    second = (rho2 * rho1, 2.0 * rho2 / DELTA)
    join = lambda x, y: jnp.where(low_lanes(x.shape), x, y)

    for source, target, (keep, scale) in ((state_a, state_b, first), (state_b, state_a, second)):
        apply(LEFT, source, lambda p: join(source[OWN, p], state_a[OUTER, p]), target, keep, scale)
        apply(OWN, source, lambda p: join(source[RIGHT, p], source[LEFT, p]), target, keep, scale)
        apply(RIGHT, source, lambda p: join(state_a[OUTER, p], source[OWN, p]), target, keep, scale)
    state_a[RIM] = join(state_a[RIGHT], state_a[LEFT])
    rhs[RIM] = join(rhs[RIGHT], rhs[LEFT])
    lanes = iota((QUADS // COMPONENTS, 4, 8, CELLS), 3)
    ends = (lanes < 32) | (lanes >= 96)
    for source, target, (keep, scale) in (
        (state_a, state_b, (None, 1.0 / THETA)),
        (state_b, state_a, first),
    ):
        apply(OWN, source, lambda p: source[RIM, p], target, keep, scale)
        apply(RIM, source, lambda p: jnp.where(ends, source[OWN, p], join(state_a[LEFT, p], state_a[RIGHT, p])), target, keep, scale)
    apply(OWN, state_a, lambda p: state_a[RIM, p], None, second[0], second[1], out)


def owner_kernel(totals, exclusive, owner):
    group, rank = lax.axis_index("group"), lax.axis_index("rank")
    devices = lax.axis_size(AXES)
    values = totals[...].astype(F32)
    rows, columns = iota(values.shape, 0), iota(values.shape, 1)
    earlier = (columns < group) | ((columns == group) & (rows < rank))
    whole = lambda x: jnp.sum(jnp.sum(x, axis=0, keepdims=True), axis=1, keepdims=True)
    before = whole(jnp.where(earlier, values, 0.0)) + exclusive[...].astype(F32)
    share = jnp.floor((whole(values) + (devices - 1.0)) * (1.0 / devices))
    place = jnp.floor(before * (1.0 / share))
    left = before - place * share
    place = place + jnp.where(left < 0.0, -1.0, jnp.where(left >= share, 1.0, 0.0))
    owner[...] = place.astype(I32)


def shards(degree, curve_order, neighbours, coupling, stiffness, lame, load):
    devices = lax.axis_size(AXES)
    ranks = lax.axis_size("rank")
    vmem = pl.BlockSpec(memory_space=pltpu.VMEM)
    row = lambda x: x.reshape(1, CELLS)
    arguments = (load.reshape(ROWS, NODES, CELLS), curve_order, row(degree), neighbours, coupling, row(stiffness), row(lame))
    arguments = tuple(pltpu.with_memory_space_constraint(x, pltpu.HBM) for x in arguments)
    packed = pl.pallas_call(
        pack_kernel,
        out_shape=(
            jax.ShapeDtypeStruct((DENSE + 2, 8, CELLS), F32),
            jax.ShapeDtypeStruct((EDGE + 2, 8, CELLS), F32),
            jax.ShapeDtypeStruct((EDGE + 2, 8, CELLS), F32),
            jax.ShapeDtypeStruct((1, CELLS), I32),
            jax.ShapeDtypeStruct((1, CELLS), I32),
        ),
        in_specs=[pl.BlockSpec(memory_space=pltpu.HBM)] * 7,
        out_specs=[vmem] * 5,
        scratch_shapes=[
            pltpu.VMEM((ROWS, 8, CELLS), F32),
            *[pltpu.VMEM(x.shape, x.dtype) for x in arguments],
            pltpu.SemaphoreType.DMA((7,)),
        ],
        compiler_params=pltpu.CompilerParams(vmem_limit_bytes=32 * 1024 * 1024),
        name="pack",
    )(*arguments)
    main, up, down, exclusive, weights = packed
    weights = lax.psum(weights, "group")
    main, up, down, weights = lax.optimization_barrier((main, up, down, weights))

    def shifted(array, by):
        pairs = [(i, i + by) for i in range(max(0, -by), min(devices, devices - by))]
        return lax.ppermute(array, AXES, pairs)

    left, right = shifted(main, 1), shifted(main, -1)
    outer_left, outer_right = shifted(up, 2), shifted(down, -2)

    totals = lax.all_to_all(jnp.broadcast_to(weights, (ranks, CELLS)), "rank", 0, 0, tiled=True)

    block = (QUADS, 4, 8, CELLS)
    smoothed = pl.pallas_call(
        smooth_kernel,
        out_shape=jax.ShapeDtypeStruct((ROWS, NODES, CELLS), F32),
        in_specs=[vmem] * 5,
        out_specs=pl.BlockSpec(memory_space=pltpu.HBM),
        cost_estimate=pl.CostEstimate(flops=7 * 10**9, bytes_accessed=10**6, transcendentals=0),
        scratch_shapes=[
            pltpu.VMEM((ROWS, NODES, CELLS), F32),
            pltpu.SemaphoreType.DMA((COMPONENTS * 6,)),
            pltpu.VMEM((5, *block), F32),
            pltpu.VMEM((5, *block), F32),
            pltpu.VMEM((5, *block), F32),
            pltpu.VMEM((5, *block), F32),
            pltpu.VMEM((5, NODES, 8, CELLS), F32),
            pltpu.VMEM((5, 3, 8, CELLS), F32),
            pltpu.VMEM((4, 6 * CELLS, CELLS), BF16),
            pltpu.VMEM((COMPONENTS, 6, 6, 8, CELLS), F32),
            pltpu.VMEM((COMPONENTS, 8, 6, 8, CELLS), F32),
            pltpu.VMEM((COMPONENTS, 8, 6, 8, CELLS), F32),
        ],
        compiler_params=pltpu.CompilerParams(vmem_limit_bytes=48 * 1024 * 1024),
        name="smooth",
    )(main, left, right, outer_left, outer_right)
    totals, smoothed = lax.optimization_barrier((totals, smoothed))
    owner = pl.pallas_call(
        owner_kernel,
        out_shape=jax.ShapeDtypeStruct((1, CELLS), I32),
        in_specs=[pl.BlockSpec(), vmem],
        out_specs=vmem,
        name="owner",
    )(totals.reshape(ranks, CELLS), exclusive)
    return owner.reshape(CELLS), smoothed.reshape(COMPONENTS, NODES, NODES, NODES, CELLS)


def solution(mesh):
    return jax.shard_map(
        shards,
        mesh=mesh,
        in_specs=(
            P(AXES),
            P(AXES, None),
            P(None, AXES),
            P(None, AXES),
            P(AXES),
            P(AXES),
            P(None, None, None, None, AXES),
        ),
        out_specs=(P(AXES), P(None, None, None, None, AXES)),
        check_vma=False,
    )
```

```python
import jax
import jax.numpy as jnp
from jax import lax
from jax.experimental import pallas as pl
from jax.experimental.pallas import tpu as pltpu
from jax.sharding import PartitionSpec as P

NODES = 6
COMPONENTS = 3
REACH = 32
SWEEPS = 2
DEGREE = 3
CELLS = 128
ROWS = COMPONENTS * NODES * NODES
QUADS = ROWS // 4
DENSE = 3 * QUADS
EDGE = 21
AXES = ("group", "rank")
THETA = (5.0 + 0.5) / 2.0
DELTA = (5.0 - 0.5) / 2.0
SIGMA = THETA / DELTA
F32, BF16, I32 = jnp.float32, jnp.bfloat16, jnp.int32


def iota(shape, dim):
    return lax.broadcasted_iota(I32, shape, dim)


def halves(x):
    high = x.astype(BF16)
    return high, (x - high.astype(F32)).astype(BF16)


def pack_kernel(*refs):
    sources, (main, up, down, exclusive, weights, padded), held, arrived = refs[:7], refs[7:13], refs[13:20], refs[20]
    copies = [pltpu.make_async_copy(a, b, arrived.at[n]) for n, (a, b) in enumerate(zip(sources, held))]
    for copy in copies:
        copy.start()
    padded[:, NODES:8, :] = jnp.zeros((ROWS, 8 - NODES, CELLS), F32)
    for copy in copies:
        copy.wait()
    load, order, degree, near, coupling, stiffness, lame = held
    padded[:, 0:NODES, :] = load[...]
    place = (iota((CELLS, CELLS), 0) == order[...]).astype(BF16)
    field = padded[...].reshape(ROWS * 8, CELLS)
    parts = jnp.concatenate(halves(field), axis=1)
    moved = jnp.dot(parts, jnp.concatenate([place, place], axis=0), preferred_element_type=F32)
    quads = moved.reshape(QUADS, 4, 8, CELLS)
    inner = iota((QUADS, 8, CELLS), 1) < NODES
    dense = [
        jnp.where(inner, quads[:, s], pltpu.roll(quads[:, 3], 6 - 2 * s, 1)) for s in range(3)
    ]
    degrees = jnp.broadcast_to(degree[...], (8, CELLS)).astype(F32).astype(BF16)
    cdeg = jnp.dot(degrees, place, preferred_element_type=F32)
    weight = (cdeg + 1.0) * (cdeg + 1.0) * (cdeg + 1.0)
    earlier = (iota((CELLS, CELLS), 0) < iota((CELLS, CELLS), 1)).astype(BF16)
    sums = jnp.dot(weight.astype(BF16), earlier, preferred_element_type=F32)
    exclusive[...] = sums[0:1].astype(I32)
    group = lax.axis_index("group")
    segment = jnp.sum(weight[0:1], axis=1, keepdims=True).astype(I32)
    weights[...] = jnp.where(iota((1, CELLS), 1) == group, segment, 0)
    lane = iota((NB, CELLS), 1)
    offset = ((near[...] - lane + 64) & (CELLS - 1)) - 64
    rows = ((lane + offset) & (2 * CELLS - 1)).astype(F32)
    small0 = jnp.concatenate([rows, stiffness[...], lame[...]], axis=0)
    small1 = jnp.concatenate([coupling[...], cdeg[0:2]], axis=0)
    for s in range(3):
        main[s * QUADS : (s + 1) * QUADS] = dense[s]
    main[DENSE] = small0
    main[DENSE + 1] = small1
    lanes = iota((EDGE, 8, CELLS), 2)
    first, last = None, None
    for s in range(4):
        count = min(EDGE, DENSE - s * EDGE)
        piece = main[s * EDGE : s * EDGE + count]
        if count < EDGE:
            piece = jnp.concatenate([piece, jnp.zeros((EDGE - count, 8, CELLS), F32)], axis=0)
        head = piece if s == 0 else pltpu.roll(piece, REACH * s, 2)
        tail = piece if s == 3 else pltpu.roll(piece, REACH * s + REACH, 2)
        if s == 0:
            first, last = head, tail
        else:
            first = jnp.where(lanes >= REACH * s, head, first)
            last = jnp.where(lanes >= REACH * s, tail, last)
    down[0:EDGE] = first
    down[EDGE] = small0
    down[EDGE + 1] = small1
    up[0:EDGE] = last
    up[EDGE] = small0
    up[EDGE + 1] = small1


NB = 6
LEFT, OWN, RIGHT, OUTER, RIM = range(5)


def spread(dense):
    sub = iota((QUADS, 8, CELLS), 1)
    parts = [dense[s * QUADS : (s + 1) * QUADS] for s in range(3)]
    zero = jnp.zeros((QUADS, 8, CELLS), F32)
    tails = [pltpu.roll(parts[s], 2 * s + 2, 1) for s in range(3)]
    fourth = jnp.where(sub < 2, tails[0], jnp.where(sub < 4, tails[1], jnp.where(sub < 6, tails[2], zero)))
    return [jnp.where(sub < NODES, part, zero) for part in parts] + [fourth]


def smooth_kernel(own, left, right, outer_left, outer_right, out,
                  results, sent, rhs, step, state_a, state_b, gain, stiff, table, couple, after_z, paired):
    low_lanes = lambda shape: iota(shape, len(shape) - 1) < 64

    for tile, source in ((LEFT, left), (OWN, own), (RIGHT, right)):
        for s, part in enumerate(spread(source[0:DENSE])):
            rhs[tile, :, s] = part
    pieces = []
    for s in range(4):
        lo = outer_right[0:EDGE] if s == 0 else pltpu.roll(outer_right[0:EDGE], CELLS - REACH * s, 2)
        hi = outer_left[0:EDGE] if s == 3 else pltpu.roll(outer_left[0:EDGE], 96 - REACH * s, 2)
        pieces.append(jnp.where(low_lanes((EDGE, 8, CELLS)), lo, hi))
    joined = jnp.concatenate(pieces, axis=0)
    for s, part in enumerate(spread(joined[0:DENSE])):
        rhs[OUTER, :, s] = part

    pick = low_lanes((8, CELLS))
    small = {
        LEFT: (left[DENSE], left[DENSE + 1]),
        OWN: (own[DENSE], own[DENSE + 1]),
        RIGHT: (right[DENSE], right[DENSE + 1]),
        OUTER: (
            jnp.where(pick, outer_right[EDGE], outer_left[EDGE]),
            jnp.where(pick, outer_right[EDGE + 1], outer_left[EDGE + 1]),
        ),
    }
    small[RIM] = tuple(jnp.where(pick, small[RIGHT][n], small[LEFT][n]) for n in range(2))
    sub = iota((8, CELLS), 0)
    for tile in range(5):
        shear, first_lame = small[tile][0][6:7], small[tile][0][7:8]
        diagonal = 1.0 / jnp.maximum(6.0 * shear + first_lame, 1e-6)
        cdeg = small[tile][1][6:7]
        for m in range(NODES):
            top = jnp.maximum(sub, m).astype(F32)
            gain[tile, m] = jnp.where(top <= cdeg, jnp.broadcast_to(diagonal, (8, CELLS)), 0.0)
        stiff[tile, 0] = jnp.broadcast_to(shear * (26.0 / 3.0), (8, CELLS))
        stiff[tile, 1] = jnp.broadcast_to(0.5 * first_lame - 20.0 * shear, (8, CELLS))
        stiff[tile, 2] = jnp.broadcast_to(0.5 * first_lame, (8, CELLS))

    def listed(tile, start, count):
        rows, weights = small[tile]
        place = (iota((count, CELLS), 0) + start).astype(F32)
        total = jnp.zeros((count, CELLS), F32)
        for k in range(NB):
            total = total + jnp.where(place == rows[k : k + 1], weights[k : k + 1], 0.0)
        return total

    inside = {tile: listed(tile, 0, CELLS) for tile in (LEFT, OWN, RIGHT)}
    across = {tile: listed(tile, CELLS, CELLS) for tile in (LEFT, OWN, RIGHT, OUTER)}
    wide = low_lanes((CELLS, CELLS))
    sides = {LEFT: (OWN, OUTER), OWN: (RIGHT, LEFT), RIGHT: (OUTER, OWN)}
    shear_of = {tile: jnp.broadcast_to(small[tile][0][6:7], (CELLS, CELLS)) for tile in range(4)}
    full = {}
    for tile, (after, before) in sides.items():
        top = inside[tile] + inside[tile].T
        bottom = across[tile] + jnp.where(wide, across[after], across[before]).T
        here = shear_of[tile]
        beside = jnp.where(wide, shear_of[after], shear_of[before])
        halved = []
        for values, other in ((top, here.T), (bottom, beside.T)):
            halved.append(values * (2.0 * here * other / jnp.maximum(here + other, 1e-6)))
        full[tile] = halved
    q = iota((CELLS, CELLS), 0)
    to_right = wide
    rim_top = jnp.where(
        to_right,
        jnp.where(q < 64, full[RIGHT][0], 0.0),
        jnp.where(q >= 64, full[LEFT][0], 0.0),
    )
    rim_bottom = jnp.where(
        to_right,
        jnp.where(q >= 96, full[RIGHT][1], jnp.where(q >= 64, full[RIGHT][0], 0.0)),
        jnp.where(q < 32, full[LEFT][1], jnp.where(q < 64, full[LEFT][0], 0.0)),
    )
    full[RIM] = [rim_top, rim_bottom]
    for slot, tile in enumerate((LEFT, OWN, RIGHT, RIM)):
        for half in range(2):
            high, low = halves(full[tile][half])
            table[slot, half * CELLS : (half + 1) * CELLS] = high
            table[slot, (2 + half) * CELLS : (3 + half) * CELLS] = high
            table[slot, (4 + half) * CELLS : (5 + half) * CELLS] = low
    slot_of = {LEFT: 0, OWN: 1, RIGHT: 2, RIM: 3}

    edge = jnp.zeros((COMPONENTS, 6, 8, CELLS), F32)
    after_z[:, 0] = edge
    after_z[:, 7] = edge
    paired[:, 0] = edge
    paired[:, 7] = edge

    def first_step(tile):
        for r in range(QUADS):
            for s in range(4):
                row = 4 * r + s
                value = gain[tile, max(row // 6 % 6, row % 6)] * rhs[tile, r, s] * (1.0 / THETA)
                step[tile, r, s] = value
                state_a[tile, r, s] = value

    for tile in (LEFT, OWN, RIGHT, OUTER):
        first_step(tile)

    def apply(tile, source, beside, target, keep, scale, final=None):
        slot = slot_of[tile]
        part = ROWS // 4 // COMPONENTS
        for a in range(COMPONENTS):
            here = source[tile, a * part : (a + 1) * part].reshape(part * 32, CELLS)
            there = beside(slice(a * part, (a + 1) * part)).reshape(part * 32, CELLS)
            (h1, l1), (h2, l2) = halves(here), halves(there)
            left_hand = jnp.concatenate([h1, h2, l1, l2, h1, h2], axis=1)
            result = jnp.dot(left_hand, table[slot], preferred_element_type=F32)
            couple[a] = result.reshape(6, 6, 8, CELLS)
            for i in range(6):
                u, y = [], []
                for j in range(6):
                    row = (a * 6 + i) * 6 + j
                    value = source[tile, row // 4, row % 4]
                    u.append(value)
                    y.append(value + 0.15 * (pltpu.roll(value, 1, 0) + pltpu.roll(value, 7, 0)))
                for j in range(6):
                    def beside_sum(values):
                        if j == 0:
                            return values[1]
                        if j == 5:
                            return values[4]
                        return values[j - 1] + values[j + 1]
                    z = y[j] + 0.15 * beside_sum(y)
                    x2 = u[j] + 0.15 * beside_sum(u)
                    after_z[a, i + 1, j] = z
                    paired[a, i + 1, j] = y[j] + x2
        k0, k1, k2 = stiff[tile, 0], stiff[tile, 1], stiff[tile, 2]
        for i in range(6):
            for j in range(6):
                ms, vs = [], []
                for a in range(COMPONENTS):
                    z = after_z[a, i + 1, j]
                    ms.append(z + 0.15 * (after_z[a, i, j] + after_z[a, i + 2, j]))
                    vs.append(z + paired[a, i + 1, j] + 0.15 * (paired[a, i, j] + paired[a, i + 2, j]))
                mixed = k2 * (ms[0] + ms[1] + ms[2])
                g = gain[tile, max(i, j)] * scale
                for a in range(COMPONENTS):
                    row = (a * 6 + i) * 6 + j
                    r, s = row // 4, row % 4
                    resid = (rhs[tile, r, s] - mixed) + (couple[a, i, j] - k0 * vs[a] - k1 * ms[a])
                    delta = g * resid
                    if keep is not None:
                        delta = delta + keep * step[tile, r, s]
                    value = source[tile, r, s] + delta
                    if final is None:
                        step[tile, r, s] = delta
                        target[tile, r, s] = value
                    else:
                        results[row] = value[0:NODES]
            if final is not None:
                for a in range(COMPONENTS):
                    rows = pl.ds((a * 6 + i) * 6, 6)
                    pltpu.make_async_copy(results.at[rows], final.at[rows], sent.at[a * 6 + i]).start()
        if final is not None:
            for n in range(COMPONENTS * 6):
                rows = pl.ds(n * 6, 6)
                pltpu.make_async_copy(results.at[rows], final.at[rows], sent.at[n]).wait()

    rho0 = 1.0 / SIGMA
    rho1 = 1.0 / (2.0 * SIGMA - rho0)
    rho2 = 1.0 / (2.0 * SIGMA - rho1)
    first = (rho1 * rho0, 2.0 * rho1 / DELTA)
    second = (rho2 * rho1, 2.0 * rho2 / DELTA)
    join = lambda x, y: jnp.where(low_lanes(x.shape), x, y)

    for source, target, (keep, scale) in ((state_a, state_b, first), (state_b, state_a, second)):
        apply(LEFT, source, lambda p: join(source[OWN, p], state_a[OUTER, p]), target, keep, scale)
        apply(OWN, source, lambda p: join(source[RIGHT, p], source[LEFT, p]), target, keep, scale)
        apply(RIGHT, source, lambda p: join(state_a[OUTER, p], source[OWN, p]), target, keep, scale)
    state_a[RIM] = join(state_a[RIGHT], state_a[LEFT])
    rhs[RIM] = join(rhs[RIGHT], rhs[LEFT])
    lanes = iota((QUADS // COMPONENTS, 4, 8, CELLS), 3)
    ends = (lanes < 32) | (lanes >= 96)
    for source, target, (keep, scale) in (
        (state_a, state_b, (None, 1.0 / THETA)),
        (state_b, state_a, first),
    ):
        apply(OWN, source, lambda p: source[RIM, p], target, keep, scale)
        apply(RIM, source, lambda p: jnp.where(ends, source[OWN, p], join(state_a[LEFT, p], state_a[RIGHT, p])), target, keep, scale)
    apply(OWN, state_a, lambda p: state_a[RIM, p], None, second[0], second[1], out)


def owner_kernel(totals, exclusive, owner):
    group, rank = lax.axis_index("group"), lax.axis_index("rank")
    devices = lax.axis_size(AXES)
    values = totals[...].astype(F32)
    rows, columns = iota(values.shape, 0), iota(values.shape, 1)
    earlier = (columns < group) | ((columns == group) & (rows < rank))
    whole = lambda x: jnp.sum(jnp.sum(x, axis=0, keepdims=True), axis=1, keepdims=True)
    before = whole(jnp.where(earlier, values, 0.0)) + exclusive[...].astype(F32)
    share = jnp.floor((whole(values) + (devices - 1.0)) * (1.0 / devices))
    place = jnp.floor(before * (1.0 / share))
    left = before - place * share
    place = place + jnp.where(left < 0.0, -1.0, jnp.where(left >= share, 1.0, 0.0))
    owner[...] = place.astype(I32)


def shards(degree, curve_order, neighbours, coupling, stiffness, lame, load):
    devices = lax.axis_size(AXES)
    ranks = lax.axis_size("rank")
    vmem = pl.BlockSpec(memory_space=pltpu.VMEM)
    row = lambda x: x.reshape(1, CELLS)
    arguments = (load.reshape(ROWS, NODES, CELLS), curve_order, row(degree), neighbours, coupling, row(stiffness), row(lame))
    arguments = tuple(pltpu.with_memory_space_constraint(x, pltpu.HBM) for x in arguments)
    packed = pl.pallas_call(
        pack_kernel,
        out_shape=(
            jax.ShapeDtypeStruct((DENSE + 2, 8, CELLS), F32),
            jax.ShapeDtypeStruct((EDGE + 2, 8, CELLS), F32),
            jax.ShapeDtypeStruct((EDGE + 2, 8, CELLS), F32),
            jax.ShapeDtypeStruct((1, CELLS), I32),
            jax.ShapeDtypeStruct((1, CELLS), I32),
        ),
        in_specs=[pl.BlockSpec(memory_space=pltpu.HBM)] * 7,
        out_specs=[vmem] * 5,
        scratch_shapes=[
            pltpu.VMEM((ROWS, 8, CELLS), F32),
            *[pltpu.VMEM(x.shape, x.dtype) for x in arguments],
            pltpu.SemaphoreType.DMA((7,)),
        ],
        compiler_params=pltpu.CompilerParams(vmem_limit_bytes=32 * 1024 * 1024),
        name="pack",
    )(*arguments)
    main, up, down, exclusive, weights = packed
    weights = lax.psum(weights, "group")
    main, up, down, weights = lax.optimization_barrier((main, up, down, weights))

    def shifted(array, by):
        pairs = [(i, i + by) for i in range(max(0, -by), min(devices, devices - by))]
        return lax.ppermute(array, AXES, pairs)

    left, right = shifted(main, 1), shifted(main, -1)
    outer_left, outer_right = shifted(up, 2), shifted(down, -2)

    totals = lax.all_to_all(jnp.broadcast_to(weights, (ranks, CELLS)), "rank", 0, 0, tiled=True)

    block = (QUADS, 4, 8, CELLS)
    smoothed = pl.pallas_call(
        smooth_kernel,
        out_shape=jax.ShapeDtypeStruct((ROWS, NODES, CELLS), F32),
        in_specs=[vmem] * 5,
        out_specs=pl.BlockSpec(memory_space=pltpu.HBM),
        cost_estimate=pl.CostEstimate(flops=10**6, bytes_accessed=10**3, transcendentals=0),
        scratch_shapes=[
            pltpu.VMEM((ROWS, NODES, CELLS), F32),
            pltpu.SemaphoreType.DMA((COMPONENTS * 6,)),
            pltpu.VMEM((5, *block), F32),
            pltpu.VMEM((5, *block), F32),
            pltpu.VMEM((5, *block), F32),
            pltpu.VMEM((5, *block), F32),
            pltpu.VMEM((5, NODES, 8, CELLS), F32),
            pltpu.VMEM((5, 3, 8, CELLS), F32),
            pltpu.VMEM((4, 6 * CELLS, CELLS), BF16),
            pltpu.VMEM((COMPONENTS, 6, 6, 8, CELLS), F32),
            pltpu.VMEM((COMPONENTS, 8, 6, 8, CELLS), F32),
            pltpu.VMEM((COMPONENTS, 8, 6, 8, CELLS), F32),
        ],
        compiler_params=pltpu.CompilerParams(vmem_limit_bytes=48 * 1024 * 1024),
        name="smooth",
    )(main, left, right, outer_left, outer_right)
    totals, smoothed = lax.optimization_barrier((totals, smoothed))
    owner = pl.pallas_call(
        owner_kernel,
        out_shape=jax.ShapeDtypeStruct((1, CELLS), I32),
        in_specs=[pl.BlockSpec(), vmem],
        out_specs=vmem,
        name="owner",
    )(totals.reshape(ranks, CELLS), exclusive)
    return owner.reshape(CELLS), smoothed.reshape(COMPONENTS, NODES, NODES, NODES, CELLS)


def solution(mesh):
    return jax.shard_map(
        shards,
        mesh=mesh,
        in_specs=(
            P(AXES),
            P(AXES, None),
            P(None, AXES),
            P(None, AXES),
            P(AXES),
            P(AXES),
            P(None, None, None, None, AXES),
        ),
        out_specs=(P(AXES), P(None, None, None, None, AXES)),
        check_vma=False,
    )
```
